256 devices in a mesh: group: 16 (over y, z_hi), space: 16 (over x, z_lo, core).
Axes of the slice: x: 4, y: 4, z: 8 (z_hi: 4, z_lo: 2; z = z_hi * 2 + z_lo), core: 2. Of those that a mesh axis runs over, the one named last changes fastest.
Arguments:
- factors: bfloat16 [16, 96, 524288], P('group', None, 'space'), may hold values from -30 to 30
Outputs:
- merged: bfloat16 [16, 96, 524288], P('group', None, 'space')
- energy: float32 [16, 96, 96], P('group')
The draws below stay inside these ranges and needn't reach their ends.
All inputs are finite; a program needn't handle non-finite values.
Results may differ from the reference program's by a relative error of at most 0.033.
Values may be sent and summed in bfloat16 or wider, within the bound.
No kernel may reach another device: no remote copies, remote signals or barrier semaphores. Data moves between devices by JAX's collectives and lax.ppermute only.
A program may use at most 128 MiB of HBM per device.

```python
import math
import jax
import jax.numpy as jnp
from jax import lax

R = 96
ITERS = 4
GROUPS = 16
ROWS = 524288


def draw_factors(key, part):
    key = jax.random.fold_in(key, 7)
    keys = jax.random.split(key, 5)
    shape_all = (GROUPS, R, ROWS)
    common = jnp.clip(jax.random.normal(keys[0], (R, ROWS), jnp.float32), -5.0, 5.0)
    private = jnp.clip(jax.random.normal(keys[1], shape_all, jnp.float32), -5.0, 5.0)
    scale_low = math.log(0.7)
    scale_high = math.log(1.4)
    neighbour = jnp.roll(common, 1, axis=0)
    position = jnp.arange(ROWS, dtype=jnp.float32) / ROWS
    amplitude = (0.4 + 1.2 * position)[None, None, :]
    weight_self = jax.random.uniform(keys[2], (GROUPS, R, 1), jnp.float32, 0.4, 1.0)
    weight_next = jax.random.uniform(keys[3], (GROUPS, R, 1), jnp.float32, -0.5, 0.5)
    column_scale = jnp.exp(jax.random.uniform(keys[4], (GROUPS, R, 1), jnp.float32, scale_low, scale_high))
    mixed = amplitude * (weight_self * common[None] + weight_next * neighbour[None]) + 0.7 * private
    return jnp.clip(column_scale * mixed, -30.0, 30.0).astype(jnp.bfloat16)


def setup_inputs(seed: int = 0) -> dict:
    arg_keys = jax.random.split(jax.random.key(seed), 2)
    factors = draw_factors(jax.random.fold_in(arg_keys[1], 71), 0)
    return dict(factors=factors)


def gram_block(left, right):
    return lax.dot_general(left.astype(jnp.float32), right.astype(jnp.float32), (((1,), (1,)), ((), ())), preferred_element_type=jnp.float32)

def orthogonal_iteration(whole_gram):
    subspace = jnp.eye(2 * R, R, dtype=jnp.float32)
    for turn_index in range(ITERS):
        image = jnp.dot(whole_gram, subspace, precision=lax.Precision.HIGHEST)
        inner = jnp.dot(image.T, image, precision=lax.Precision.HIGHEST)
        lower_factor = jnp.linalg.cholesky(inner)
        subspace = jax.scipy.linalg.solve_triangular(lower_factor, image.T, lower=True).T
    energy = jnp.dot(subspace.T, jnp.dot(whole_gram, subspace, precision=lax.Precision.HIGHEST), precision=lax.Precision.HIGHEST) / ROWS
    return (subspace, energy)

def reference(factors):
    current = [factors[index] for index in range(GROUPS)]
    energies = [None] * GROUPS
    for section_bit in (0, 1):
        distance = 1 << section_bit
        updated = [None] * GROUPS
        for group_index in range(GROUPS):
            partner_index = group_index ^ distance
            if group_index < partner_index:
                stacked = jnp.concatenate([current[group_index], current[partner_index]], axis=0)
                whole_gram = gram_block(stacked, stacked)
                subspace, energy = orthogonal_iteration(whole_gram)
                coefficients = subspace.astype(jnp.bfloat16)
                result = lax.dot_general(coefficients.astype(jnp.float32), stacked.astype(jnp.float32), (((0,), (0,)), ((), ())), preferred_element_type=jnp.float32).astype(jnp.bfloat16)
                updated[group_index] = result
                updated[partner_index] = result
                energies[group_index] = energy
                energies[partner_index] = energy
        current = updated
    return (jnp.stack(current, axis=0), jnp.stack(energies, axis=0))
```

```python
import jax
import jax.numpy as jnp
from jax import lax
from jax.sharding import Mesh, PartitionSpec as P

ITERS = 4
HIGHEST = lax.Precision.HIGHEST


def pair_swap(x, axis):
    return lax.ppermute(x, axis, [(0, 1), (1, 0)])


def shifted(x, axis, step):
    n = lax.axis_size(axis)
    return lax.ppermute(x, axis, [(i, (i + step) % n) for i in range(n)])


def scatter_pair(x, axis):
    me = lax.axis_index(axis)
    low, high = jnp.split(x, 2, axis=0)
    keep = jnp.where(me == 0, low, high)
    give = jnp.where(me == 0, high, low)
    return keep + pair_swap(give, axis)


def gather_pair(x, axis):
    me = lax.axis_index(axis)
    other = pair_swap(x, axis)
    return jnp.concatenate([jnp.where(me == 0, x, other), jnp.where(me == 0, other, x)], axis=0)


def scatter_ring(x, axis):
    n = lax.axis_size(axis)
    me = lax.axis_index(axis)
    rows = x.shape[0] // n
    pieces = x.reshape(n, rows, x.shape[1])

    def piece(step):
        return lax.dynamic_index_in_dim(pieces, (me + step) % n, 0, keepdims=False)

    got = [shifted(piece(step), axis, step) for step in range(1, n)]
    return sum(got, piece(0))


def gather_ring(x, axis):
    n = lax.axis_size(axis)
    me = lax.axis_index(axis)
    got = [x] + [shifted(x, axis, step) for step in range(1, n)]
    stack = jnp.stack(got)
    order = (me - jnp.arange(n)) % n
    return stack[order].reshape(n * x.shape[0], x.shape[1])


def sum_ring(x, axis):
    n = lax.axis_size(axis)
    return sum([shifted(x, axis, step) for step in range(1, n)], x)


def sum_gram(gram):
    packed = jnp.concatenate(
        [gram[128 * i : 128 * i + 128, 128 * j : 128 * j + 128] for i in range(3) for j in range(i, 3)],
        axis=0,
    )
    part = scatter_pair(packed, "core")
    part = scatter_pair(part, "z_lo")
    part = scatter_ring(part, "x")
    part = sum_ring(part, "z_hi")
    part = gather_ring(part, "x")
    part = gather_pair(part, "z_lo")
    packed = gather_pair(part, "core").reshape(6, 128, 128)
    place = {}
    count = 0
    for i in range(3):
        for j in range(i, 3):
            place[i, j] = packed[count]
            if i != j:
                place[j, i] = packed[count].T
            count += 1
    return jnp.concatenate(
        [jnp.concatenate([place[i, j] for j in range(3)], axis=1) for i in range(3)], axis=0
    )


def orthogonal_iteration(whole_gram):
    rank = whole_gram.shape[0] // 2
    subspace = jnp.eye(2 * rank, rank, dtype=jnp.float32)
    for turn_index in range(ITERS):
        image = jnp.dot(whole_gram, subspace, precision=HIGHEST)
        inner = jnp.dot(image.T, image, precision=HIGHEST)
        lower_factor = jnp.linalg.cholesky(inner)
        subspace = jax.scipy.linalg.solve_triangular(lower_factor, image.T, lower=True).T
    return subspace


def solve(gram, row_total):
    half = gram.shape[0] // 2
    low = orthogonal_iteration(gram[:half, :half]).astype(jnp.bfloat16).astype(jnp.float32)
    high = orthogonal_iteration(gram[half:, half:]).astype(jnp.bfloat16).astype(jnp.float32)
    zero = jnp.zeros_like(low)
    first = jnp.concatenate(
        [jnp.concatenate([low, zero], axis=1), jnp.concatenate([zero, high], axis=1)], axis=0
    )
    second_gram = jnp.dot(first.T, jnp.dot(gram, first, precision=HIGHEST), precision=HIGHEST)
    subspace = orthogonal_iteration(second_gram)
    energy = (
        jnp.dot(subspace.T, jnp.dot(second_gram, subspace, precision=HIGHEST), precision=HIGHEST)
        / row_total
    )
    second = subspace.astype(jnp.bfloat16).astype(jnp.float32)
    return jnp.dot(first, second, precision=HIGHEST).astype(jnp.bfloat16), energy


def local(factors):
    own = factors[0]
    row_total = own.shape[1] * lax.axis_size(("x", "z_lo", "core"))
    rows = lax.all_to_all(own, "z_hi", 1, 0, tiled=True)
    gram = lax.dot_general(rows, rows, (((1,), (1,)), ((), ())), preferred_element_type=jnp.float32)
    coef, energy = solve(sum_gram(gram), row_total)
    merged = lax.dot_general(
        coef, rows, (((0,), (0,)), ((), ())), preferred_element_type=jnp.float32
    ).astype(jnp.bfloat16)
    merged = lax.all_gather(merged, "z_hi", axis=1, tiled=True)
    return (merged[None], energy[None])


def solution(mesh):
    fine = Mesh(mesh.devices.reshape(4, 4, 4, 2, 2), ("y", "z_hi", "x", "z_lo", "core"))
    group, space = ("y", "z_hi"), ("x", "z_lo", "core")
    return jax.shard_map(
        local,
        mesh=fine,
        in_specs=(P(group, None, space),),
        out_specs=(P(group, None, space), P(group, None, None)),
        check_vma=False,
    )
```

```python
import functools

import jax
import jax.numpy as jnp
from jax import lax
from jax.experimental import pallas as pl
from jax.experimental.pallas import tpu as pltpu
from jax.sharding import Mesh, PartitionSpec as P

ITERS = 4
RANK = 96
LANES = 128
HIGHEST = lax.Precision.HIGHEST


def dot(a, b, contract, precision=HIGHEST):
    return lax.dot_general(
        a, b, (contract, ((), ())), precision=precision, preferred_element_type=jnp.float32
    )


def invert_factors(works):
    eight = (8, LANES)
    sublane = lax.broadcasted_iota(jnp.int32, (8, 2 * LANES), 0)
    for block in range(RANK // 8):
        top = 8 * block
        for work in works:
            panel = work[top : top + 8, :]
            a = {
                (i, j): jnp.broadcast_to(panel[i : i + 1, top + j : top + j + 1], eight)
                for i in range(8)
                for j in range(i + 1)
            }
            rows = [jnp.broadcast_to(panel[i : i + 1, :], (8, 2 * LANES)) for i in range(8)]
            done = jnp.zeros((8, 2 * LANES), jnp.float32)
            for j in range(8):
                inverse = 1.0 / a[j, j]
                root = lax.rsqrt(a[j, j])
                scaled = rows[j] * jnp.concatenate([root, root], axis=1)
                done = jnp.where(sublane == j, scaled, done)
                for i in range(j + 1, 8):
                    factor = a[i, j] * inverse
                    for k in range(j + 1, i + 1):
                        a[i, k] = a[i, k] - factor * a[k, j]
                    rows[i] = rows[i] - jnp.concatenate([factor, factor], axis=1) * rows[j]
            work[top : top + 8, :] = done
            if top + 8 < RANK:
                change = dot(done[:, :LANES], done, ((0,), (0,)))
                work[top + 8 : RANK, :] = work[top + 8 : RANK, :] - change[top + 8 : RANK, :]


def iterate(grams, images, subspaces, works):
    row = lax.broadcasted_iota(jnp.int32, (RANK, LANES), 0)
    column = lax.broadcasted_iota(jnp.int32, (RANK, LANES), 1)
    identity = jnp.where(row == column, 1.0, 0.0).astype(jnp.float32)
    empty = jnp.zeros((LANES - RANK, LANES), jnp.float32)

    def turn(index, carry):
        for image, work in zip(images, works):
            held = image[...]
            work[:, :LANES] = dot(held, held, ((0,), (0,)))[:RANK]
            work[:, LANES:] = identity
        ahead = [dot(gram[...], image[...], ((1,), (0,))) for gram, image in zip(grams, images)]
        invert_factors(works)
        for image, subspace, work, product in zip(images, subspaces, works, ahead):
            inverse = jnp.concatenate([work[:, LANES:], empty], axis=0)
            subspace[...] = dot(image[...], inverse, ((1,), (1,)))
            image[...] = dot(product, inverse, ((1,), (1,)))
        return carry

    lax.fori_loop(0, ITERS, turn, 0)


def solver_body(
    row_total, gram_ref, coef_ref, energy_ref, gram_a, gram_b, image_a, image_b, sub_a, sub_b,
    work_a, work_b, gram_c, image_c, sub_c,
):
    half = 2 * RANK
    lane = lax.broadcasted_iota(jnp.int32, (half, LANES), 1)
    for index, (gram, image) in enumerate(((gram_a, image_a), (gram_b, image_b))):
        block = gram_ref[half * index : half * index + half, half * index : half * index + half]
        gram[...] = block
        image[...] = jnp.where(lane < RANK, block[:, :LANES], 0.0)
    iterate((gram_a, gram_b), (image_a, image_b), (sub_a, sub_b), (work_a, work_b))
    first_a = sub_a[...].astype(jnp.bfloat16)
    first_b = sub_b[...].astype(jnp.bfloat16)
    wide_a, wide_b = first_a.astype(jnp.float32), first_b.astype(jnp.float32)
    side_a = dot(gram_a[...], wide_a, ((1,), (0,)))
    side_b = dot(gram_b[...], wide_b, ((1,), (0,)))
    cross = dot(gram_ref[half:, :half], wide_a, ((1,), (0,)))
    low_left = dot(wide_b, cross, ((0,), (0,)))
    gram_c[:LANES, :LANES] = dot(wide_a, side_a, ((0,), (0,)))
    gram_c[LANES:, LANES:] = dot(wide_b, side_b, ((0,), (0,)))
    gram_c[LANES:, :LANES] = low_left
    gram_c[:LANES, LANES:] = low_left.T
    image_c[...] = gram_c[:, :LANES]
    iterate((gram_c,), (image_c,), (sub_c,), (work_a,))
    final = sub_c[...]
    energy = dot(final, dot(gram_c[...], final, ((1,), (0,))), ((0,), (0,)))
    energy_ref[...] = energy[:RANK, :RANK] * (1.0 / row_total)
    second = final.astype(jnp.bfloat16)
    coef_ref[:half, :] = dot(first_a, second[:LANES], ((1,), (0,)), None)[:, :RANK].astype(jnp.bfloat16)
    coef_ref[half:, :] = dot(first_b, second[LANES:], ((1,), (0,)), None)[:, :RANK].astype(jnp.bfloat16)


def solve(gram, row_total):
    f32 = jnp.float32
    half, wide = 2 * RANK, 2 * LANES
    return pl.pallas_call(
        functools.partial(solver_body, row_total),
        out_shape=(
            jax.ShapeDtypeStruct((2 * half, RANK), jnp.bfloat16),
            jax.ShapeDtypeStruct((RANK, RANK), f32),
        ),
        in_specs=[pl.BlockSpec(memory_space=pltpu.VMEM)],
        out_specs=(pl.BlockSpec(memory_space=pltpu.VMEM),) * 2,
        scratch_shapes=[
            pltpu.VMEM((half, half), f32), pltpu.VMEM((half, half), f32),
            pltpu.VMEM((half, LANES), f32), pltpu.VMEM((half, LANES), f32),
            pltpu.VMEM((half, LANES), f32), pltpu.VMEM((half, LANES), f32),
            pltpu.VMEM((RANK, wide), f32), pltpu.VMEM((RANK, wide), f32),
            pltpu.VMEM((wide, wide), f32), pltpu.VMEM((wide, LANES), f32), pltpu.VMEM((wide, LANES), f32),
        ],
        compiler_params=pltpu.CompilerParams(vmem_limit_bytes=32 * 1024 * 1024),
        name="solver",
    )(gram)


def pair_swap(x, axis):
    return lax.ppermute(x, axis, [(0, 1), (1, 0)])


def shifted(x, axis, step):
    n = lax.axis_size(axis)
    return lax.ppermute(x, axis, [(i, (i + step) % n) for i in range(n)])


def scatter_pair(x, axis):
    me = lax.axis_index(axis)
    low, high = jnp.split(x, 2, axis=0)
    keep = jnp.where(me == 0, low, high)
    give = jnp.where(me == 0, high, low)
    return keep + pair_swap(give, axis)


def gather_pair(x, axis):
    me = lax.axis_index(axis)
    other = pair_swap(x, axis)
    return jnp.concatenate([jnp.where(me == 0, x, other), jnp.where(me == 0, other, x)], axis=0)


def scatter_ring(x, axis):
    n = lax.axis_size(axis)
    me = lax.axis_index(axis)
    rows = x.shape[0] // n
    pieces = x.reshape(n, rows, x.shape[1])

    def piece(step):
        return lax.dynamic_index_in_dim(pieces, (me + step) % n, 0, keepdims=False)

    got = [shifted(piece(step), axis, step) for step in range(1, n)]
    return sum(got, piece(0))


def gather_ring(x, axis):
    n = lax.axis_size(axis)
    me = lax.axis_index(axis)
    got = [x] + [shifted(x, axis, step) for step in range(1, n)]
    stack = jnp.stack(got)
    order = (me - jnp.arange(n)) % n
    return stack[order].reshape(n * x.shape[0], x.shape[1])


def sum_ring(x, axis):
    n = lax.axis_size(axis)
    return sum([shifted(x, axis, step) for step in range(1, n)], x)


def sum_gram(gram):
    packed = jnp.concatenate(
        [gram[128 * i : 128 * i + 128, 128 * j : 128 * j + 128] for i in range(3) for j in range(i, 3)],
        axis=0,
    )
    part = scatter_pair(packed, "core")
    part = scatter_pair(part, "z_lo")
    part = scatter_ring(part, "x")
    part = sum_ring(part, "z_hi")
    part = gather_ring(part, "x")
    part = gather_pair(part, "z_lo")
    packed = gather_pair(part, "core").reshape(6, 128, 128)
    place = {}
    count = 0
    for i in range(3):
        for j in range(i, 3):
            place[i, j] = packed[count]
            if i != j:
                place[j, i] = packed[count].T
            count += 1
    return jnp.concatenate(
        [jnp.concatenate([place[i, j] for j in range(3)], axis=1) for i in range(3)], axis=0
    )


def cut(whole, starts, width):
    return [lax.dynamic_slice_in_dim(whole, start * width, width, 1) for start in starts]


def place(pieces, starts, whole):
    width = pieces[0].shape[1]
    for piece, start in zip(pieces, starts):
        whole = lax.dynamic_update_slice_in_dim(whole, piece, start * width, 1)
    return whole


def gram_body(*refs):
    pieces, gram_ref, held = refs[:8], refs[8], refs[9]
    rank, width = pieces[0].shape
    for index in range(8):
        row, column = index % 4 * rank, index // 4 * width
        held[row : row + rank, column : column + width] = pieces[index][...]
    product = lax.dot_general(
        held[...], held[...], (((1,), (1,)), ((), ())), preferred_element_type=jnp.float32
    )

    @pl.when(pl.program_id(0) == 0)
    def _():
        gram_ref[...] = product

    @pl.when(pl.program_id(0) > 0)
    def _():
        gram_ref[...] = gram_ref[...] + product


def local_gram(pieces):
    rank, columns = pieces[0].shape
    width = min(columns, 1024)
    return pl.pallas_call(
        gram_body,
        out_shape=jax.ShapeDtypeStruct((4 * rank, 4 * rank), jnp.float32),
        grid=(columns // width,),
        in_specs=[pl.BlockSpec((rank, width), lambda i: (0, i))] * 8,
        out_specs=pl.BlockSpec((4 * rank, 4 * rank), lambda i: (0, 0)),
        scratch_shapes=[pltpu.VMEM((4 * rank, 2 * width), jnp.bfloat16)],
        cost_estimate=pl.CostEstimate(
            flops=64 * rank * rank * columns, bytes_accessed=16 * rank * columns, transcendentals=0
        ),
        compiler_params=pltpu.CompilerParams(vmem_limit_bytes=32 * 1024 * 1024),
        name="local_gram",
    )(*pieces)


def merge_body(sets, *refs):
    coef_ref, pieces, outs, held = refs[0], refs[1 : 1 + 4 * sets], refs[1 + 4 * sets : -1], refs[-1]
    rank = pieces[0].shape[0]
    for index in range(sets):
        for row in range(4):
            held[row * rank : row * rank + rank, :] = pieces[4 * index + row][...]
        outs[index][...] = jnp.dot(
            coef_ref[...], held[...], preferred_element_type=jnp.float32
        ).astype(jnp.bfloat16)


def merge(coef, sets):
    count = len(sets)
    rank, columns = sets[0][0].shape
    width = min(columns, 1024)
    block = pl.BlockSpec((rank, width), lambda i: (0, i))
    return pl.pallas_call(
        functools.partial(merge_body, count),
        out_shape=(jax.ShapeDtypeStruct((rank, columns), jnp.bfloat16),) * count,
        grid=(columns // width,),
        in_specs=[pl.BlockSpec((rank, 4 * rank), lambda i: (0, 0))] + [block] * (4 * count),
        out_specs=(block,) * count,
        scratch_shapes=[pltpu.VMEM((4 * rank, width), jnp.bfloat16)],
        cost_estimate=pl.CostEstimate(
            flops=8 * count * rank * rank * columns,
            bytes_accessed=10 * count * rank * columns,
            transcendentals=0,
        ),
        compiler_params=pltpu.CompilerParams(vmem_limit_bytes=32 * 1024 * 1024),
        name="merge",
    )(coef, *[piece for pieces in sets for piece in pieces])


def up(x):
    return shifted(x, "z_hi", 1)


def down(x):
    return shifted(x, "z_hi", -1)


def local(factors):
    own = factors[0]
    rank, columns = own.shape
    row_total = columns * lax.axis_size(("x", "z_lo", "core"))
    me = lax.axis_index("z_hi")
    width = columns // 8

    def spot(step, half):
        return (me + step) % 4 * 2 + half

    def part(*spots):
        return cut(own, [spot(*s) for s in spots], width)

    far_down, far_up = part((2, 0), (1, 1))
    below_first, above_second, below_second, above_first, kept_first, kept_second = part(
        (3, 0), (0, 1), (2, 1), (1, 0), (0, 0), (3, 1)
    )
    a2 = down(far_down)
    b2 = up(far_up)
    a1 = down(below_first)
    b1 = up(above_second)
    a3 = down(below_second)
    b3 = up(above_first)
    a4 = down(a2)
    b4 = up(b2)
    gram = local_gram([kept_first, a1, a4, b3, kept_second, a3, b4, b1])
    gram = jnp.roll(gram, (rank * me, rank * me), (0, 1))
    gram = sum_gram(gram)
    gram, kept_first, kept_second, b3, a3 = lax.optimization_barrier(
        (gram, kept_first, kept_second, b3, a3)
    )
    c1 = up(kept_first)
    c3 = down(kept_second)
    c2 = up(b3)
    c4 = down(a3)
    coef, energy = solve(gram, float(row_total))
    coef = jnp.roll(coef, -rank * me, 0).T
    upper_first, upper_second, lower_first, lower_second = merge(
        coef,
        [
            [kept_first, a1, a4, b3],
            [above_second, c3, c4, b2],
            [below_first, a2, c2, c1],
            [kept_second, a3, b4, b1],
        ],
    )
    sent = [down(upper_first), up(lower_first), down(upper_second), up(lower_second)]
    merged = jnp.zeros((rank, columns), jnp.bfloat16)
    merged = place(
        [upper_first, upper_second, lower_first, lower_second],
        [spot(0, 0), spot(0, 1), spot(3, 0), spot(3, 1)],
        merged,
    )
    merged = place(sent, [spot(1, 0), spot(2, 0), spot(1, 1), spot(2, 1)], merged)
    return (merged[None], energy[None])


def solution(mesh):
    sizes = mesh.devices.size // 64
    fine = Mesh(mesh.devices.reshape(sizes, 4, 4, 2, 2), ("y", "z_hi", "x", "z_lo", "core"))
    group, space = ("y", "z_hi"), ("x", "z_lo", "core")
    return jax.shard_map(
        local,
        mesh=fine,
        in_specs=(P(group, None, space),),
        out_specs=(P(group, None, space), P(group, None, None)),
        check_vma=False,
    )
```

```python
import functools

import jax
import jax.numpy as jnp
from jax import lax
from jax.experimental import pallas as pl
from jax.experimental.pallas import tpu as pltpu
from jax.sharding import Mesh, PartitionSpec as P

ITERS = 4
RANK = 96
LANES = 128
HIGHEST = lax.Precision.HIGHEST


def dot(a, b, contract, precision=HIGHEST):
    return lax.dot_general(
        a, b, (contract, ((), ())), precision=precision, preferred_element_type=jnp.float32
    )


def invert_factors(works):
    eight = (8, LANES)
    sublane = lax.broadcasted_iota(jnp.int32, (8, LANES), 0)
    tiles = (0, LANES)
    for block in range(RANK // 8):
        top = 8 * block
        for work in works:
            panel = work[top : top + 8, :]
            a = {
                (i, j): jnp.broadcast_to(panel[i : i + 1, top + j : top + j + 1], eight)
                for i in range(8)
                for j in range(i + 1)
            }
            inverse = []
            for j in range(8):
                inverse.append(1.0 / a[j, j])
                for i in range(j + 1, 8):
                    factor = a[i, j] * inverse[j]
                    for k in range(j + 1, i + 1):
                        a[i, k] = a[i, k] - factor * a[k, j]
            rows = [
                [jnp.broadcast_to(panel[i : i + 1, t : t + LANES], eight) for t in tiles]
                for i in range(8)
            ]
            done = [jnp.zeros(eight, jnp.float32) for t in tiles]
            for j in range(8):
                root = lax.rsqrt(a[j, j])
                done = [jnp.where(sublane == j, row * root, d) for row, d in zip(rows[j], done)]
                for i in range(j + 1, 8):
                    factor = a[i, j] * inverse[j]
                    rows[i] = [row - factor * pivot for row, pivot in zip(rows[i], rows[j])]
            for t, d in zip(tiles, done):
                work[top : top + 8, t : t + LANES] = d
            for row in range(top + 8, RANK, 8):
                rest = [work[row : row + 8, t : t + LANES] for t in tiles]
                column = [jnp.broadcast_to(rest[0][:, top + j : top + j + 1], eight) for j in range(8)]
                for j in range(8):
                    factor = column[j] * inverse[j]
                    for k in range(j + 1, 8):
                        column[k] = column[k] - factor * a[k, j]
                    rest = [r - factor * pivot for r, pivot in zip(rest, rows[j])]
                for t, r in zip(tiles, rest):
                    work[row : row + 8, t : t + LANES] = r


def iterate(grams, images, works):
    row = lax.broadcasted_iota(jnp.int32, (RANK, LANES), 0)
    column = lax.broadcasted_iota(jnp.int32, (RANK, LANES), 1)
    identity = jnp.where(row == column, 1.0, 0.0).astype(jnp.float32)
    empty = jnp.zeros((LANES - RANK, LANES), jnp.float32)

    def turn(index, carry):
        now, later = lax.rem(index, 2), lax.rem(index + 1, 2)
        for image, work in zip(images, works):
            held = image[now]
            work[:, :LANES] = dot(held, held, ((0,), (0,)))[:RANK]
            work[:, LANES:] = identity
        ahead = [dot(gram[...], image[now], ((1,), (0,))) for gram, image in zip(grams, images)]
        invert_factors(works)
        for image, work, product in zip(images, works, ahead):
            inverse = jnp.concatenate([work[:, LANES:], empty], axis=0)
            image[later] = dot(product, inverse, ((1,), (1,)))
        return carry

    lax.fori_loop(0, ITERS, turn, 0)
    found = []
    for image, work in zip(images, works):
        inverse = jnp.concatenate([work[:, LANES:], empty], axis=0)
        found.append(dot(image[(ITERS - 1) % 2], inverse, ((1,), (1,))))
    return found


def solver_body(
    row_total, place_ref, own_ref, other_ref, coef_ref, energy_ref, gram_a, gram_b, image_a, image_b,
    work_a, work_b, gram_c, image_c, gram_ref,
):
    half = 2 * RANK
    first = place_ref[1] == 0
    count = 0
    for i in range(3):
        for j in range(i, 3):
            here = slice(LANES * (count % 3), LANES * (count % 3 + 1))
            own, other = own_ref[here, :], other_ref[here, :]
            tile = jnp.where(first, own, other) if count < 3 else jnp.where(first, other, own)
            gram_ref[LANES * i : LANES * (i + 1), LANES * j : LANES * (j + 1)] = tile
            if i != j:
                gram_ref[LANES * j : LANES * (j + 1), LANES * i : LANES * (i + 1)] = tile.T
            count += 1
    lane = lax.broadcasted_iota(jnp.int32, (half, LANES), 1)
    for index, (gram, image) in enumerate(((gram_a, image_a), (gram_b, image_b))):
        block = gram_ref[half * index : half * index + half, half * index : half * index + half]
        gram[...] = block
        image[0] = jnp.where(lane < RANK, block[:, :LANES], 0.0)
    first_a, first_b = [
        found.astype(jnp.bfloat16)
        for found in iterate((gram_a, gram_b), (image_a, image_b), (work_a, work_b))
    ]
    wide_a, wide_b = first_a.astype(jnp.float32), first_b.astype(jnp.float32)
    side_a = dot(gram_a[...], wide_a, ((1,), (0,)))
    side_b = dot(gram_b[...], wide_b, ((1,), (0,)))
    cross = dot(gram_ref[half:, :half], wide_a, ((1,), (0,)))
    low_left = dot(wide_b, cross, ((0,), (0,)))
    gram_c[:LANES, :LANES] = dot(wide_a, side_a, ((0,), (0,)))
    gram_c[LANES:, LANES:] = dot(wide_b, side_b, ((0,), (0,)))
    gram_c[LANES:, :LANES] = low_left
    gram_c[:LANES, LANES:] = low_left.T
    image_c[0] = gram_c[:, :LANES]
    (final,) = iterate((gram_c,), (image_c,), (work_a,))
    energy = dot(final, dot(gram_c[...], final, ((1,), (0,))), ((0,), (0,)))
    energy_ref[...] = energy[:RANK, :RANK] * (1.0 / row_total)
    second = final.astype(jnp.bfloat16)
    coef_ref[:, :half] = dot(second[:LANES], first_a, ((0,), (1,)), None)[:RANK].astype(jnp.bfloat16)
    coef_ref[:, half:] = dot(second[LANES:], first_b, ((0,), (1,)), None)[:RANK].astype(jnp.bfloat16)


def solve(halves, places, row_total):
    f32 = jnp.float32
    half, wide = 2 * RANK, 2 * LANES
    return pl.pallas_call(
        functools.partial(solver_body, row_total),
        out_shape=(
            jax.ShapeDtypeStruct((RANK, 2 * half), jnp.bfloat16),
            jax.ShapeDtypeStruct((RANK, RANK), f32),
        ),
        in_specs=[pl.BlockSpec(memory_space=pltpu.SMEM)] + [pl.BlockSpec(memory_space=pltpu.VMEM)] * 2,
        out_specs=(pl.BlockSpec(memory_space=pltpu.VMEM),) * 2,
        scratch_shapes=[
            pltpu.VMEM((half, half), f32), pltpu.VMEM((half, half), f32),
            pltpu.VMEM((2, half, LANES), f32), pltpu.VMEM((2, half, LANES), f32),
            pltpu.VMEM((RANK, wide), f32), pltpu.VMEM((RANK, wide), f32),
            pltpu.VMEM((wide, wide), f32), pltpu.VMEM((2, wide, LANES), f32),
            pltpu.VMEM((2 * half, 2 * half), f32),
        ],
        compiler_params=pltpu.CompilerParams(vmem_limit_bytes=32 * 1024 * 1024),
        name="solver",
    )(places, *halves)


def pair_swap(x, axis):
    return lax.ppermute(x, axis, [(0, 1), (1, 0)])


def shifted(x, axis, step):
    n = lax.axis_size(axis)
    return lax.ppermute(x, axis, [(i, (i + step) % n) for i in range(n)])


def sum_ring(x, axis):
    n = lax.axis_size(axis)
    return sum([shifted(x, axis, step) for step in range(1, n)], x)


def ring_sum_pp(x):
    n = lax.axis_size("x")
    me = lax.axis_index("x")
    rows = x.shape[0] // n
    pieces = x.reshape(n, rows, x.shape[1])

    def piece(step):
        return lax.dynamic_index_in_dim(pieces, (me + step) % n, 0, keepdims=False)

    got = [shifted(piece(step), "x", step) for step in range(1, n)]
    mine = sum_ring(sum(got, piece(0)), "z_hi")
    got = [mine] + [shifted(mine, "x", step) for step in range(1, n)]
    return jnp.stack(got)[(me - jnp.arange(n)) % n].reshape(x.shape)


def sum_halves(keep, give):
    part = keep + pair_swap(give, "core")
    part = part + pair_swap(part, "z_lo")
    part = ring_sum_pp(part)
    return part, pair_swap(part, "core")


def cut(whole, starts, width):
    return [lax.dynamic_slice_in_dim(whole, start * width, width, 1) for start in starts]


def place(pieces, starts, whole):
    width = pieces[0].shape[1]
    for piece, start in zip(pieces, starts):
        whole = lax.dynamic_update_slice_in_dim(whole, piece, start * width, 1)
    return whole


PAIRS = [(i, j) for i in range(3) for j in range(i, 3)]


def ring_row(place_ref, step, rank):
    return pl.multiple_of(lax.rem(place_ref[0] + step, 4) * rank, 32)


def gram_body(steps, place_ref, *refs):
    pieces, keep_ref, give_ref, held, total = refs[:8], *refs[8:]
    rank, width = pieces[0].shape
    for index in range(8):
        row, column = ring_row(place_ref, index % 4, rank), index // 4 * width
        held[pl.ds(row, rank), column : column + width] = pieces[index][...]
    product = lax.dot_general(
        held[...], held[...], (((1,), (1,)), ((), ())), preferred_element_type=jnp.float32
    )

    @pl.when(pl.program_id(0) == 0)
    def _():
        total[...] = product

    @pl.when(pl.program_id(0) > 0)
    def _():
        total[...] = total[...] + product

    @pl.when(pl.program_id(0) == steps - 1)
    def _():
        first = place_ref[1] == 0
        for index in range(3):
            (i, j), (k, m) = PAIRS[index], PAIRS[index + 3]
            low = total[LANES * i : LANES * (i + 1), LANES * j : LANES * (j + 1)]
            high = total[LANES * k : LANES * (k + 1), LANES * m : LANES * (m + 1)]
            here = slice(LANES * index, LANES * (index + 1))
            keep_ref[here, :] = jnp.where(first, low, high)
            give_ref[here, :] = jnp.where(first, high, low)


def local_gram(pieces, places):
    rank, columns = pieces[0].shape
    width = min(columns, 1024)
    steps = columns // width
    half = jax.ShapeDtypeStruct((3 * LANES, LANES), jnp.float32)
    half_spec = pl.BlockSpec((3 * LANES, LANES), lambda i: (0, 0))
    return pl.pallas_call(
        functools.partial(gram_body, steps),
        out_shape=(half, half),
        grid=(steps,),
        in_specs=[pl.BlockSpec(memory_space=pltpu.SMEM)]
        + [pl.BlockSpec((rank, width), lambda i: (0, i))] * 8,
        out_specs=(half_spec, half_spec),
        scratch_shapes=[
            pltpu.VMEM((4 * rank, 2 * width), jnp.bfloat16),
            pltpu.VMEM((4 * rank, 4 * rank), jnp.float32),
        ],
        cost_estimate=pl.CostEstimate(
            flops=64 * rank * rank * columns, bytes_accessed=16 * rank * columns, transcendentals=0
        ),
        compiler_params=pltpu.CompilerParams(vmem_limit_bytes=32 * 1024 * 1024),
        name="local_gram",
    )(places, *pieces)


def merge_body(sets, place_ref, coef_ref, *refs):
    pieces, outs, held = refs[: 4 * sets], refs[4 * sets : -1], refs[-1]
    rank = pieces[0].shape[0]
    for index in range(sets):
        for row in range(4):
            held[pl.ds(ring_row(place_ref, row, rank), rank), :] = pieces[4 * index + row][...]
        outs[index][...] = jnp.dot(
            coef_ref[...], held[...], preferred_element_type=jnp.float32
        ).astype(jnp.bfloat16)


def merge(coef, sets, places):
    count = len(sets)
    rank, columns = sets[0][0].shape
    width = min(columns, 1024)
    block = pl.BlockSpec((rank, width), lambda i: (0, i))
    return pl.pallas_call(
        functools.partial(merge_body, count),
        out_shape=(jax.ShapeDtypeStruct((rank, columns), jnp.bfloat16),) * count,
        grid=(columns // width,),
        in_specs=[
            pl.BlockSpec(memory_space=pltpu.SMEM),
            pl.BlockSpec((rank, 4 * rank), lambda i: (0, 0)),
        ]
        + [block] * (4 * count),
        out_specs=(block,) * count,
        scratch_shapes=[pltpu.VMEM((4 * rank, width), jnp.bfloat16)],
        cost_estimate=pl.CostEstimate(
            flops=8 * count * rank * rank * columns,
            bytes_accessed=10 * count * rank * columns,
            transcendentals=0,
        ),
        compiler_params=pltpu.CompilerParams(vmem_limit_bytes=32 * 1024 * 1024),
        name="merge",
    )(places, coef, *[piece for pieces in sets for piece in pieces])


def up(x):
    return shifted(x, "z_hi", 1)


def down(x):
    return shifted(x, "z_hi", -1)


def local(factors):
    own = factors[0]
    rank, columns = own.shape
    row_total = columns * lax.axis_size(("x", "z_lo", "core"))
    me = lax.axis_index("z_hi")
    width = columns // 8

    def spot(step, half):
        return (me + step) % 4 * 2 + half

    def part(*spots):
        return cut(own, [spot(*s) for s in spots], width)

    far_down, far_up = part((2, 0), (1, 1))
    below_first, above_second, below_second, above_first, kept_first, kept_second = part(
        (3, 0), (0, 1), (2, 1), (1, 0), (0, 0), (3, 1)
    )
    a2 = down(far_down)
    b2 = up(far_up)
    a1 = down(below_first)
    b1 = up(above_second)
    a3 = down(below_second)
    b3 = up(above_first)
    a4 = down(a2)
    b4 = up(b2)
    places = jnp.stack([me, lax.axis_index("core")]).astype(jnp.int32)
    halves = local_gram([kept_first, a1, a4, b3, kept_second, a3, b4, b1], places)
    halves = sum_halves(*halves)
    c1 = up(kept_first)
    c3 = down(kept_second)
    c2 = up(b3)
    c4 = down(a3)
    coef, energy = solve(halves, places, float(row_total))
    upper_first, upper_second, lower_first, lower_second = merge(
        coef,
        [
            [kept_first, a1, a4, b3],
            [above_second, c3, c4, b2],
            [below_first, a2, c2, c1],
            [kept_second, a3, b4, b1],
        ],
        places,
    )
    sent = [down(upper_first), up(lower_first), down(upper_second), up(lower_second)]
    merged = jnp.zeros((rank, columns), jnp.bfloat16)
    merged = place(
        [upper_first, upper_second, lower_first, lower_second],
        [spot(0, 0), spot(0, 1), spot(3, 0), spot(3, 1)],
        merged,
    )
    merged = place(sent, [spot(1, 0), spot(2, 0), spot(1, 1), spot(2, 1)], merged)
    return (merged[None], energy[None])


def solution(mesh):
    sizes = mesh.devices.size // 64
    fine = Mesh(mesh.devices.reshape(sizes, 4, 4, 2, 2), ("y", "z_hi", "x", "z_lo", "core"))
    group, space = ("y", "z_hi"), ("x", "z_lo", "core")
    return jax.shard_map(
        local,
        mesh=fine,
        in_specs=(P(group, None, space),),
        out_specs=(P(group, None, space), P(group, None, None)),
        check_vma=False,
    )
```

```python
import functools

import jax
import jax.numpy as jnp
from jax import lax
from jax.experimental import pallas as pl
from jax.experimental.pallas import tpu as pltpu
from jax.sharding import Mesh, PartitionSpec as P

ITERS = 4
RANK = 96
LANES = 128
HIGHEST = lax.Precision.HIGHEST


def dot(a, b, contract, precision=HIGHEST):
    return lax.dot_general(
        a, b, (contract, ((), ())), precision=precision, preferred_element_type=jnp.float32
    )


def invert_factors(works):
    eight = (8, LANES)
    sublane = lax.broadcasted_iota(jnp.int32, eight, 0)
    lane = lax.broadcasted_iota(jnp.int32, eight, 1)
    for top in range(0, RANK, 8):
        inside = (lane >= top) & (lane < top + 8)
        for work in works:
            panel = work[top : top + 8, :]
            a = {
                (i, j): jnp.broadcast_to(panel[i : i + 1, top + j : top + j + 1], eight)
                for i in range(8)
                for j in range(i + 1)
            }
            inverse = []
            for j in range(8):
                inverse.append(1.0 / a[j, j])
                for i in range(j + 1, 8):
                    factor = a[i, j] * inverse[j]
                    for k in range(j + 1, i + 1):
                        a[i, k] = a[i, k] - factor * a[k, j]
            opened = jnp.where(inside, jnp.where(lane == top + sublane, 1.0, 0.0), panel)
            rows = [jnp.broadcast_to(opened[i : i + 1], eight) for i in range(8)]
            done = rows[0] * lax.rsqrt(a[0, 0])
            for j in range(8):
                if j > 0:
                    done = jnp.where(sublane == j, rows[j] * lax.rsqrt(a[j, j]), done)
                for i in range(j + 1, 8):
                    rows[i] = rows[i] - (a[i, j] * inverse[j]) * rows[j]
            work[top : top + 8, :] = done
            if top + 8 == RANK:
                continue
            held = work[top + 8 : top + 16, :]
            column = [jnp.broadcast_to(held[:, top + j : top + j + 1], eight) for j in range(8)]
            held = jnp.where(inside, 0.0, held)
            for j in range(8):
                factor = column[j] * inverse[j]
                for k in range(j + 1, 8):
                    column[k] = column[k] - factor * a[k, j]
                held = held - factor * rows[j]
            work[top + 8 : top + 16, :] = held
            if top + 16 < RANK and len(works) > 1:
                change = dot(done, done, ((0,), (0,)))
                for row in range(top + 16, RANK, 8):
                    rest = jnp.where(inside, 0.0, work[row : row + 8, :])
                    work[row : row + 8, :] = rest - change[row : row + 8, :]
            elif top + 16 < RANK:
                for row in range(top + 16, RANK, 8):
                    held = work[row : row + 8, :]
                    column = [jnp.broadcast_to(held[:, top + j : top + j + 1], eight) for j in range(8)]
                    held = jnp.where(inside, 0.0, held)
                    for j in range(8):
                        factor = column[j] * inverse[j]
                        for k in range(j + 1, 8):
                            column[k] = column[k] - factor * a[k, j]
                        held = held - factor * rows[j]
                    work[row : row + 8, :] = held


def iterate(grams, images, works):
    row = lax.broadcasted_iota(jnp.int32, (RANK, LANES), 0)
    column = lax.broadcasted_iota(jnp.int32, (RANK, LANES), 1)
    lower = row >= column
    empty = jnp.zeros((LANES - RANK, LANES), jnp.float32)

    def turn(index, carry):
        now, later = lax.rem(index, 2), lax.rem(index + 1, 2)
        for image, work in zip(images, works):
            held = image[now]
            work[...] = dot(held, held, ((0,), (0,)))[:RANK]
        ahead = [dot(gram[...], image[now], ((1,), (0,))) for gram, image in zip(grams, images)]
        invert_factors(works)
        for image, work, product in zip(images, works, ahead):
            inverse = jnp.concatenate([jnp.where(lower, work[...], 0.0), empty], axis=0)
            image[later] = dot(product, inverse, ((1,), (1,)))
        return carry

    lax.fori_loop(0, ITERS, turn, 0)
    found = []
    for image, work in zip(images, works):
        inverse = jnp.concatenate([jnp.where(lower, work[...], 0.0), empty], axis=0)
        found.append(dot(image[(ITERS - 1) % 2], inverse, ((1,), (1,))))
    return found


def solver_body(
    row_total, place_ref, own_ref, other_ref, coef_ref, energy_ref, gram_a, gram_b, image_a, image_b,
    work_a, work_b, gram_c, image_c, gram_ref,
):
    half = 2 * RANK
    first = place_ref[1] == 0
    count = 0
    for i in range(3):
        for j in range(i, 3):
            here = slice(LANES * (count % 3), LANES * (count % 3 + 1))
            own, other = own_ref[here, :], other_ref[here, :]
            tile = jnp.where(first, own, other) if count < 3 else jnp.where(first, other, own)
            gram_ref[LANES * i : LANES * (i + 1), LANES * j : LANES * (j + 1)] = tile
            if i != j:
                gram_ref[LANES * j : LANES * (j + 1), LANES * i : LANES * (i + 1)] = tile.T
            count += 1
    lane = lax.broadcasted_iota(jnp.int32, (half, LANES), 1)
    for index, (gram, image) in enumerate(((gram_a, image_a), (gram_b, image_b))):
        block = gram_ref[half * index : half * index + half, half * index : half * index + half]
        gram[...] = block
        image[0] = jnp.where(lane < RANK, block[:, :LANES], 0.0)
    first_a, first_b = [
        found.astype(jnp.bfloat16)
        for found in iterate((gram_a, gram_b), (image_a, image_b), (work_a, work_b))
    ]
    wide_a, wide_b = first_a.astype(jnp.float32), first_b.astype(jnp.float32)
    side_a = dot(gram_a[...], wide_a, ((1,), (0,)))
    side_b = dot(gram_b[...], wide_b, ((1,), (0,)))
    cross = dot(gram_ref[half:, :half], wide_a, ((1,), (0,)))
    low_left = dot(wide_b, cross, ((0,), (0,)))
    gram_c[:LANES, :LANES] = dot(wide_a, side_a, ((0,), (0,)))
    gram_c[LANES:, LANES:] = dot(wide_b, side_b, ((0,), (0,)))
    gram_c[LANES:, :LANES] = low_left
    gram_c[:LANES, LANES:] = low_left.T
    image_c[0] = gram_c[:, :LANES]
    (final,) = iterate((gram_c,), (image_c,), (work_a,))
    energy = dot(final, dot(gram_c[...], final, ((1,), (0,))), ((0,), (0,)))
    energy_ref[...] = energy[:RANK, :RANK] * (1.0 / row_total)
    second = final.astype(jnp.bfloat16)
    coef_ref[:, :half] = dot(second[:LANES], first_a, ((0,), (1,)), None)[:RANK].astype(jnp.bfloat16)
    coef_ref[:, half:] = dot(second[LANES:], first_b, ((0,), (1,)), None)[:RANK].astype(jnp.bfloat16)


def solve(halves, places, row_total):
    f32 = jnp.float32
    half, wide = 2 * RANK, 2 * LANES
    return pl.pallas_call(
        functools.partial(solver_body, row_total),
        out_shape=(
            jax.ShapeDtypeStruct((RANK, 2 * half), jnp.bfloat16),
            jax.ShapeDtypeStruct((RANK, RANK), f32),
        ),
        in_specs=[pl.BlockSpec(memory_space=pltpu.SMEM)] + [pl.BlockSpec(memory_space=pltpu.VMEM)] * 2,
        out_specs=(pl.BlockSpec(memory_space=pltpu.VMEM),) * 2,
        scratch_shapes=[
            pltpu.VMEM((half, half), f32), pltpu.VMEM((half, half), f32),
            pltpu.VMEM((2, half, LANES), f32), pltpu.VMEM((2, half, LANES), f32),
            pltpu.VMEM((RANK, LANES), f32), pltpu.VMEM((RANK, LANES), f32),
            pltpu.VMEM((wide, wide), f32), pltpu.VMEM((2, wide, LANES), f32),
            pltpu.VMEM((2 * half, 2 * half), f32),
        ],
        compiler_params=pltpu.CompilerParams(vmem_limit_bytes=32 * 1024 * 1024),
        name="solver",
    )(places, *halves)


def pair_swap(x, axis):
    return lax.ppermute(x, axis, [(0, 1), (1, 0)])


def shifted(x, axis, step):
    n = lax.axis_size(axis)
    return lax.ppermute(x, axis, [(i, (i + step) % n) for i in range(n)])


def sum_halves(keep, give, riders):
    part = keep + pair_swap(give, "core")
    n = lax.axis_size("x")
    me = lax.axis_index("x")
    pieces = part.reshape(n, part.shape[0] // n, part.shape[1])

    def piece(step):
        return lax.dynamic_index_in_dim(pieces, (me + step) % n, 0, keepdims=False)

    mine = sum([shifted(piece(step), "x", step) for step in range(1, n)], piece(0))
    mine = mine + pair_swap(mine, "z_lo")
    with jax.named_scope("ring_sum"):
        got = [shifted(mine, "z_hi", step) for step in range(1, lax.axis_size("z_hi"))]
    got, riders = lax.optimization_barrier((got, riders))
    mine = sum(got, mine)
    got = [mine] + [shifted(mine, "x", step) for step in range(1, n)]
    part = jnp.stack(got)[(me - jnp.arange(n)) % n].reshape(part.shape)
    return (part, pair_swap(part, "core")), riders


def cut(whole, starts, width):
    return [lax.dynamic_slice_in_dim(whole, start * width, width, 1) for start in starts]


def place(pieces, starts, whole):
    width = pieces[0].shape[1]
    for piece, start in zip(pieces, starts):
        whole = lax.dynamic_update_slice_in_dim(whole, piece, start * width, 1)
    return whole


PAIRS = [(i, j) for i in range(3) for j in range(i, 3)]


def ring_row(place_ref, step, rank):
    return pl.multiple_of(lax.rem(place_ref[0] + step, 4) * rank, 32)


def gram_body(width, place_ref, *refs):
    pieces, keep_ref, give_ref, held, total = refs[:8], *refs[8:]
    rank, columns = pieces[0].shape
    for step in range(columns // width):
        for index in range(8):
            row, column = ring_row(place_ref, index % 4, rank), index // 4 * width
            block = pieces[index][:, width * step : width * step + width]
            held[step % 2, pl.ds(row, rank), column : column + width] = block
        rows = held[step % 2]
        product = lax.dot_general(
            rows, rows, (((1,), (1,)), ((), ())), preferred_element_type=jnp.float32
        )
        total[...] = product if step == 0 else total[...] + product
    first = place_ref[1] == 0
    for index in range(3):
        (i, j), (k, m) = PAIRS[index], PAIRS[index + 3]
        low = total[LANES * i : LANES * (i + 1), LANES * j : LANES * (j + 1)]
        high = total[LANES * k : LANES * (k + 1), LANES * m : LANES * (m + 1)]
        here = slice(LANES * index, LANES * (index + 1))
        keep_ref[here, :] = jnp.where(first, low, high)
        give_ref[here, :] = jnp.where(first, high, low)


def local_gram(pieces, places):
    rank, columns = pieces[0].shape
    width = min(columns, 1024)
    half = jax.ShapeDtypeStruct((3 * LANES, LANES), jnp.float32)
    whole = pl.BlockSpec(memory_space=pltpu.VMEM)
    return pl.pallas_call(
        functools.partial(gram_body, width),
        out_shape=(half, half),
        in_specs=[pl.BlockSpec(memory_space=pltpu.SMEM)] + [whole] * 8,
        out_specs=(whole, whole),
        scratch_shapes=[
            pltpu.VMEM((2, 4 * rank, 2 * width), jnp.bfloat16),
            pltpu.VMEM((4 * rank, 4 * rank), jnp.float32),
        ],
        cost_estimate=pl.CostEstimate(
            flops=64 * rank * rank * columns, bytes_accessed=16 * rank * columns, transcendentals=0
        ),
        compiler_params=pltpu.CompilerParams(vmem_limit_bytes=48 * 1024 * 1024),
        name="local_gram",
    )(places, *pieces)


def merge_body(sets, width, place_ref, coef_ref, *refs):
    pieces, outs, held = refs[: 4 * sets], refs[4 * sets : -1], refs[-1]
    rank, columns = pieces[0].shape
    slot = 0
    for index in range(sets):
        for step in range(columns // width):
            here = slice(width * step, width * step + width)
            for row in range(4):
                spot = pl.ds(ring_row(place_ref, row, rank), rank)
                held[slot, spot, :] = pieces[4 * index + row][:, here]
            outs[index][:, here] = jnp.dot(
                coef_ref[...], held[slot], preferred_element_type=jnp.float32
            ).astype(jnp.bfloat16)
            slot = 1 - slot


def merge(coef, sets, places):
    count = len(sets)
    rank, columns = sets[0][0].shape
    width = min(columns, 1024)
    whole = pl.BlockSpec(memory_space=pltpu.VMEM)
    return pl.pallas_call(
        functools.partial(merge_body, count, width),
        out_shape=(jax.ShapeDtypeStruct((rank, columns), jnp.bfloat16),) * count,
        in_specs=[pl.BlockSpec(memory_space=pltpu.SMEM)] + [whole] * (1 + 4 * count),
        out_specs=(whole,) * count,
        scratch_shapes=[pltpu.VMEM((2, 4 * rank, width), jnp.bfloat16)],
        cost_estimate=pl.CostEstimate(
            flops=8 * count * rank * rank * columns,
            bytes_accessed=10 * count * rank * columns,
            transcendentals=0,
        ),
        compiler_params=pltpu.CompilerParams(vmem_limit_bytes=48 * 1024 * 1024),
        name="merge",
    )(places, coef, *[piece for pieces in sets for piece in pieces])


def up(x):
    return shifted(x, "z_hi", 1)


def down(x):
    return shifted(x, "z_hi", -1)


def local(factors):
    own = factors[0]
    rank, columns = own.shape
    row_total = columns * lax.axis_size(("x", "z_lo", "core"))
    me = lax.axis_index("z_hi")
    width = columns // 8

    def spot(step, half):
        return (me + step) % 4 * 2 + half

    def part(*spots):
        return cut(own, [spot(*s) for s in spots], width)

    far_down, far_up = part((2, 0), (1, 1))
    a2 = down(far_down)
    b2 = up(far_up)
    own, far_down, far_up = lax.optimization_barrier((own, far_down, far_up))
    below_first, above_second, below_second, above_first, kept_first, kept_second = part(
        (3, 0), (0, 1), (2, 1), (1, 0), (0, 0), (3, 1)
    )
    a1 = down(below_first)
    b1 = up(above_second)
    a2, below_late = lax.optimization_barrier((a2, below_second))
    a4 = down(a2)
    a3 = down(below_late)
    b2, above_late = lax.optimization_barrier((b2, above_first))
    b4 = up(b2)
    b3 = up(above_late)
    places = jnp.stack([me, lax.axis_index("core")]).astype(jnp.int32)
    halves = local_gram([kept_first, a1, a4, b3, kept_second, a3, b4, b1], places)
    halves, (kept_first, kept_second, b3, a3) = sum_halves(
        *halves, (kept_first, kept_second, b3, a3)
    )
    with jax.named_scope("second_holder"):
        c1 = up(kept_first)
        c3 = down(kept_second)
        c2 = up(b3)
        c4 = down(a3)
    coef, energy = solve(halves, places, float(row_total))
    coef, c1, c3 = lax.optimization_barrier((coef, c1, c3))
    upper_first, lower_second = merge(
        coef, [[kept_first, a1, a4, b3], [kept_second, a3, b4, b1]], places
    )
    with jax.named_scope("result"):
        sent_first, sent_second = down(upper_first), up(lower_second)
    upper_second, lower_first = merge(
        coef, [[above_second, c3, c4, b2], [below_first, a2, c2, c1]], places
    )
    with jax.named_scope("result"):
        sent = [sent_first, sent_second, up(lower_first), down(upper_second)]
    merged = jnp.zeros((rank, columns), jnp.bfloat16)
    merged = place(sent[:2], [spot(1, 0), spot(2, 1)], merged)
    merged = place(
        [upper_first, upper_second, lower_first, lower_second],
        [spot(0, 0), spot(0, 1), spot(3, 0), spot(3, 1)],
        merged,
    )
    merged = place(sent[2:], [spot(2, 0), spot(1, 1)], merged)
    return (merged[None], energy[None])


def solution(mesh):
    sizes = mesh.devices.size // 64
    fine = Mesh(mesh.devices.reshape(sizes, 4, 4, 2, 2), ("y", "z_hi", "x", "z_lo", "core"))
    group, space = ("y", "z_hi"), ("x", "z_lo", "core")
    return jax.shard_map(
        local,
        mesh=fine,
        in_specs=(P(group, None, space),),
        out_specs=(P(group, None, space), P(group, None, None)),
        check_vma=False,
    )
```

```python
import functools

import jax
import jax.numpy as jnp
from jax import lax
from jax.experimental import pallas as pl
from jax.experimental.pallas import tpu as pltpu
from jax.sharding import Mesh, PartitionSpec as P

ITERS = 4
RANK = 96
LANES = 128
HIGHEST = lax.Precision.HIGHEST


def dot(a, b, contract, precision=HIGHEST):
    return lax.dot_general(
        a, b, (contract, ((), ())), precision=precision, preferred_element_type=jnp.float32
    )


def invert_factors(works):
    eight = (8, LANES)
    sublane = lax.broadcasted_iota(jnp.int32, eight, 0)
    lane = lax.broadcasted_iota(jnp.int32, eight, 1)
    for top in range(0, RANK, 8):
        inside = (lane >= top) & (lane < top + 8)
        for work in works:
            panel = work[top : top + 8, :]
            a = {
                (i, j): jnp.broadcast_to(panel[i : i + 1, top + j : top + j + 1], eight)
                for i in range(8)
                for j in range(i + 1)
            }
            inverse = []
            for j in range(8):
                inverse.append(1.0 / a[j, j])
                for i in range(j + 1, 8):
                    factor = a[i, j] * inverse[j]
                    for k in range(j + 1, i + 1):
                        a[i, k] = a[i, k] - factor * a[k, j]
            opened = jnp.where(inside, jnp.where(lane == top + sublane, 1.0, 0.0), panel)
            rows = [jnp.broadcast_to(opened[i : i + 1], eight) for i in range(8)]
            done = rows[0] * lax.rsqrt(a[0, 0])
            for j in range(8):
                if j > 0:
                    done = jnp.where(sublane == j, rows[j] * lax.rsqrt(a[j, j]), done)
                for i in range(j + 1, 8):
                    rows[i] = rows[i] - (a[i, j] * inverse[j]) * rows[j]
            work[top : top + 8, :] = done
            if top + 8 == RANK:
                continue
            held = work[top + 8 : top + 16, :]
            column = [jnp.broadcast_to(held[:, top + j : top + j + 1], eight) for j in range(8)]
            held = jnp.where(inside, 0.0, held)
            for j in range(8):
                factor = column[j] * inverse[j]
                for k in range(j + 1, 8):
                    column[k] = column[k] - factor * a[k, j]
                held = held - factor * rows[j]
            work[top + 8 : top + 16, :] = held
            if top + 16 < RANK and len(works) > 1:
                change = dot(done, done, ((0,), (0,)))
                for row in range(top + 16, RANK, 8):
                    rest = jnp.where(inside, 0.0, work[row : row + 8, :])
                    work[row : row + 8, :] = rest - change[row : row + 8, :]
            elif top + 16 < RANK:
                for row in range(top + 16, RANK, 8):
                    held = work[row : row + 8, :]
                    column = [jnp.broadcast_to(held[:, top + j : top + j + 1], eight) for j in range(8)]
                    held = jnp.where(inside, 0.0, held)
                    for j in range(8):
                        factor = column[j] * inverse[j]
                        for k in range(j + 1, 8):
                            column[k] = column[k] - factor * a[k, j]
                        held = held - factor * rows[j]
                    work[row : row + 8, :] = held


def iterate(grams, images, works):
    row = lax.broadcasted_iota(jnp.int32, (RANK, LANES), 0)
    column = lax.broadcasted_iota(jnp.int32, (RANK, LANES), 1)
    lower = row >= column
    empty = jnp.zeros((LANES - RANK, LANES), jnp.float32)

    def turn(index, carry):
        now, later = lax.rem(index, 2), lax.rem(index + 1, 2)
        for image, work in zip(images, works):
            held = image[now]
            work[...] = dot(held, held, ((0,), (0,)))[:RANK]
        ahead = [dot(gram[...], image[now], ((1,), (0,))) for gram, image in zip(grams, images)]
        invert_factors(works)
        for image, work, product in zip(images, works, ahead):
            inverse = jnp.concatenate([jnp.where(lower, work[...], 0.0), empty], axis=0)
            image[later] = dot(product, inverse, ((1,), (1,)))
        return carry

    lax.fori_loop(0, ITERS, turn, 0)
    found = []
    for image, work in zip(images, works):
        inverse = jnp.concatenate([jnp.where(lower, work[...], 0.0), empty], axis=0)
        found.append(dot(image[(ITERS - 1) % 2], inverse, ((1,), (1,))))
    return found


def solver_body(
    row_total, place_ref, own_ref, other_ref, coef_ref, energy_ref, gram_a, gram_b, image_a, image_b,
    work_a, work_b, gram_c, image_c, gram_ref,
):
    half = 2 * RANK
    first = place_ref[1] == 0
    count = 0
    for i in range(3):
        for j in range(i, 3):
            here = slice(LANES * (count % 3), LANES * (count % 3 + 1))
            own, other = own_ref[here, :], other_ref[here, :]
            tile = jnp.where(first, own, other) if count < 3 else jnp.where(first, other, own)
            gram_ref[LANES * i : LANES * (i + 1), LANES * j : LANES * (j + 1)] = tile
            if i != j:
                gram_ref[LANES * j : LANES * (j + 1), LANES * i : LANES * (i + 1)] = tile.T
            count += 1
    lane = lax.broadcasted_iota(jnp.int32, (half, LANES), 1)
    for index, (gram, image) in enumerate(((gram_a, image_a), (gram_b, image_b))):
        block = gram_ref[half * index : half * index + half, half * index : half * index + half]
        gram[...] = block
        image[0] = jnp.where(lane < RANK, block[:, :LANES], 0.0)
    first_a, first_b = [
        found.astype(jnp.bfloat16)
        for found in iterate((gram_a, gram_b), (image_a, image_b), (work_a, work_b))
    ]
    wide_a, wide_b = first_a.astype(jnp.float32), first_b.astype(jnp.float32)
    side_a = dot(gram_a[...], wide_a, ((1,), (0,)))
    side_b = dot(gram_b[...], wide_b, ((1,), (0,)))
    cross = dot(gram_ref[half:, :half], wide_a, ((1,), (0,)))
    low_left = dot(wide_b, cross, ((0,), (0,)))
    gram_c[:LANES, :LANES] = dot(wide_a, side_a, ((0,), (0,)))
    gram_c[LANES:, LANES:] = dot(wide_b, side_b, ((0,), (0,)))
    gram_c[LANES:, :LANES] = low_left
    gram_c[:LANES, LANES:] = low_left.T
    image_c[0] = gram_c[:, :LANES]
    (final,) = iterate((gram_c,), (image_c,), (work_a,))
    energy = dot(final, dot(gram_c[...], final, ((1,), (0,))), ((0,), (0,)))
    energy_ref[...] = energy[:RANK, :RANK] * (1.0 / row_total)
    second = final.astype(jnp.bfloat16)
    coef_ref[:, :half] = dot(second[:LANES], first_a, ((0,), (1,)), None)[:RANK].astype(jnp.bfloat16)
    coef_ref[:, half:] = dot(second[LANES:], first_b, ((0,), (1,)), None)[:RANK].astype(jnp.bfloat16)


def solve(halves, places, row_total):
    f32 = jnp.float32
    half, wide = 2 * RANK, 2 * LANES
    return pl.pallas_call(
        functools.partial(solver_body, row_total),
        out_shape=(
            jax.ShapeDtypeStruct((RANK, 2 * half), jnp.bfloat16),
            jax.ShapeDtypeStruct((RANK, RANK), f32),
        ),
        in_specs=[pl.BlockSpec(memory_space=pltpu.SMEM)] + [pl.BlockSpec(memory_space=pltpu.VMEM)] * 2,
        out_specs=(pl.BlockSpec(memory_space=pltpu.VMEM),) * 2,
        scratch_shapes=[
            pltpu.VMEM((half, half), f32), pltpu.VMEM((half, half), f32),
            pltpu.VMEM((2, half, LANES), f32), pltpu.VMEM((2, half, LANES), f32),
            pltpu.VMEM((RANK, LANES), f32), pltpu.VMEM((RANK, LANES), f32),
            pltpu.VMEM((wide, wide), f32), pltpu.VMEM((2, wide, LANES), f32),
            pltpu.VMEM((2 * half, 2 * half), f32),
        ],
        compiler_params=pltpu.CompilerParams(vmem_limit_bytes=32 * 1024 * 1024),
        name="solver",
    )(places, *halves)


def pair_swap(x, axis):
    return lax.ppermute(x, axis, [(0, 1), (1, 0)])


def shifted(x, axis, step):
    n = lax.axis_size(axis)
    return lax.ppermute(x, axis, [(i, (i + step) % n) for i in range(n)])


def sum_halves(keep, give, riders):
    part = keep + pair_swap(give, "core")
    n = lax.axis_size("x")
    me = lax.axis_index("x")
    pieces = part.reshape(n, part.shape[0] // n, part.shape[1])

    def piece(step):
        return lax.dynamic_index_in_dim(pieces, (me + step) % n, 0, keepdims=False)

    mine = sum([shifted(piece(step), "x", step) for step in range(1, n)], piece(0))
    mine = mine + pair_swap(mine, "z_lo")
    with jax.named_scope("ring_sum"):
        got = [shifted(mine, "z_hi", step) for step in range(1, lax.axis_size("z_hi"))]
    got, riders = lax.optimization_barrier((got, riders))
    mine = sum(got, mine)
    got = [mine] + [shifted(mine, "x", step) for step in range(1, n)]
    part = jnp.stack(got)[(me - jnp.arange(n)) % n].reshape(part.shape)
    return (part, pair_swap(part, "core")), riders


def cut(whole, starts, width):
    return [lax.dynamic_slice_in_dim(whole, start * width, width, 1) for start in starts]


def place(pieces, starts, whole):
    width = pieces[0].shape[1]
    for piece, start in zip(pieces, starts):
        whole = lax.dynamic_update_slice_in_dim(whole, piece, start * width, 1)
    return whole


PAIRS = [(i, j) for i in range(3) for j in range(i, 3)]


def ring_row(place_ref, step, rank):
    return pl.multiple_of(lax.rem(place_ref[0] + step, 4) * rank, 32)


def add_gram(first, width, place_ref, pieces, held, total_ref):
    rank, columns = pieces[0].shape
    for step in range(columns // width):
        for index in range(4):
            spot = pl.ds(ring_row(place_ref, index, rank), rank)
            held[step % 2, spot, :] = pieces[index][:, width * step : width * step + width]
        rows = held[step % 2]
        product = lax.dot_general(
            rows, rows, (((1,), (1,)), ((), ())), preferred_element_type=jnp.float32
        )
        total_ref[...] = product if first and step == 0 else total_ref[...] + product


def first_gram_body(width, place_ref, *refs):
    pieces, total_ref, held = refs[:4], *refs[4:]
    add_gram(True, width, place_ref, pieces, held, total_ref)


def last_gram_body(width, place_ref, before_ref, *refs):
    pieces, keep_ref, give_ref, held, total = refs[:4], *refs[4:]
    total[...] = before_ref[...]
    add_gram(False, width, place_ref, pieces, held, total)
    first = place_ref[1] == 0
    for index in range(3):
        (i, j), (k, m) = PAIRS[index], PAIRS[index + 3]
        low = total[LANES * i : LANES * (i + 1), LANES * j : LANES * (j + 1)]
        high = total[LANES * k : LANES * (k + 1), LANES * m : LANES * (m + 1)]
        here = slice(LANES * index, LANES * (index + 1))
        keep_ref[here, :] = jnp.where(first, low, high)
        give_ref[here, :] = jnp.where(first, high, low)


def local_gram(pieces, places, before=None):
    rank, columns = pieces[0].shape
    width = min(columns, 2048)
    square = jax.ShapeDtypeStruct((4 * rank, 4 * rank), jnp.float32)
    half = jax.ShapeDtypeStruct((3 * LANES, LANES), jnp.float32)
    whole = pl.BlockSpec(memory_space=pltpu.VMEM)
    held = pltpu.VMEM((2, 4 * rank, width), jnp.bfloat16)
    start = before is None
    operands = list(pieces) if start else [before, *pieces]
    return pl.pallas_call(
        functools.partial(first_gram_body if start else last_gram_body, width),
        out_shape=square if start else (half, half),
        in_specs=[pl.BlockSpec(memory_space=pltpu.SMEM)] + [whole] * len(operands),
        out_specs=whole if start else (whole, whole),
        scratch_shapes=[held] if start else [held, pltpu.VMEM(square.shape, jnp.float32)],
        cost_estimate=pl.CostEstimate(
            flops=32 * rank * rank * columns, bytes_accessed=8 * rank * columns, transcendentals=0
        ),
        compiler_params=pltpu.CompilerParams(vmem_limit_bytes=48 * 1024 * 1024),
        name="local_gram",
    )(places, *operands)


def merge_body(sets, width, place_ref, coef_ref, *refs):
    pieces, outs, held = refs[: 4 * sets], refs[4 * sets : -1], refs[-1]
    rank, columns = pieces[0].shape
    slot = 0
    for index in range(sets):
        for step in range(columns // width):
            here = slice(width * step, width * step + width)
            for row in range(4):
                spot = pl.ds(ring_row(place_ref, row, rank), rank)
                held[slot, spot, :] = pieces[4 * index + row][:, here]
            outs[index][:, here] = jnp.dot(
                coef_ref[...], held[slot], preferred_element_type=jnp.float32
            ).astype(jnp.bfloat16)
            slot = 1 - slot


def merge(coef, sets, places):
    count = len(sets)
    rank, columns = sets[0][0].shape
    width = min(columns, 1024)
    whole = pl.BlockSpec(memory_space=pltpu.VMEM)
    return pl.pallas_call(
        functools.partial(merge_body, count, width),
        out_shape=(jax.ShapeDtypeStruct((rank, columns), jnp.bfloat16),) * count,
        in_specs=[pl.BlockSpec(memory_space=pltpu.SMEM)] + [whole] * (1 + 4 * count),
        out_specs=(whole,) * count,
        scratch_shapes=[pltpu.VMEM((2, 4 * rank, width), jnp.bfloat16)],
        cost_estimate=pl.CostEstimate(
            flops=8 * count * rank * rank * columns,
            bytes_accessed=10 * count * rank * columns,
            transcendentals=0,
        ),
        compiler_params=pltpu.CompilerParams(vmem_limit_bytes=48 * 1024 * 1024),
        name="merge",
    )(places, coef, *[piece for pieces in sets for piece in pieces])


def up(x):
    return shifted(x, "z_hi", 1)


def down(x):
    return shifted(x, "z_hi", -1)


def local(factors):
    own = factors[0]
    rank, columns = own.shape
    row_total = columns * lax.axis_size(("x", "z_lo", "core"))
    me = lax.axis_index("z_hi")
    width = columns // 8

    def spot(step, half):
        return (me + step) % 4 * 2 + half

    def part(*spots):
        return cut(own, [spot(*s) for s in spots], width)

    far_down, far_up = part((2, 0), (1, 1))
    a2 = down(far_down)
    b2 = up(far_up)
    own, far_down, far_up = lax.optimization_barrier((own, far_down, far_up))
    below_first, above_second = part((3, 0), (0, 1))
    a1 = down(below_first)
    b1 = up(above_second)
    a2, own_late = lax.optimization_barrier((a2, own))
    below_second, kept_first, kept_second = cut(
        own_late, [spot(2, 1), spot(0, 0), spot(3, 1)], width
    )
    a4 = down(a2)
    a3 = down(below_second)
    b2, own_late = lax.optimization_barrier((b2, own))
    (above_first,) = cut(own_late, [spot(1, 0)], width)
    b4 = up(b2)
    b3 = up(above_first)
    places = jnp.stack([me, lax.axis_index("core")]).astype(jnp.int32)
    before = local_gram([kept_first, a1, a4, b3], places)
    halves = local_gram([kept_second, a3, b4, b1], places, before)
    halves, (kept_first, kept_second, b3, a3) = sum_halves(
        *halves, (kept_first, kept_second, b3, a3)
    )
    with jax.named_scope("second_holder"):
        c1 = up(kept_first)
        c3 = down(kept_second)
        c2 = up(b3)
        c4 = down(a3)
    coef, energy = solve(halves, places, float(row_total))
    coef, c1, c3 = lax.optimization_barrier((coef, c1, c3))
    upper_first, lower_second = merge(
        coef, [[kept_first, a1, a4, b3], [kept_second, a3, b4, b1]], places
    )
    with jax.named_scope("result"):
        sent_first, sent_second = down(upper_first), up(lower_second)
    upper_second, lower_first = merge(
        coef, [[above_second, c3, c4, b2], [below_first, a2, c2, c1]], places
    )
    with jax.named_scope("result"):
        sent = [sent_first, sent_second, up(lower_first), down(upper_second)]
    merged = jnp.zeros((rank, columns), jnp.bfloat16)
    merged = place(sent[:2], [spot(1, 0), spot(2, 1)], merged)
    merged = place(
        [upper_first, upper_second, lower_first, lower_second],
        [spot(0, 0), spot(0, 1), spot(3, 0), spot(3, 1)],
        merged,
    )
    merged = place(sent[2:], [spot(2, 0), spot(1, 1)], merged)
    return (merged[None], energy[None])


def solution(mesh):
    sizes = mesh.devices.size // 64
    fine = Mesh(mesh.devices.reshape(sizes, 4, 4, 2, 2), ("y", "z_hi", "x", "z_lo", "core"))
    group, space = ("y", "z_hi"), ("x", "z_lo", "core")
    return jax.shard_map(
        local,
        mesh=fine,
        in_specs=(P(group, None, space),),
        out_specs=(P(group, None, space), P(group, None, None)),
        check_vma=False,
    )
```

```python
import functools

import jax
import jax.numpy as jnp
from jax import lax
from jax.experimental import pallas as pl
from jax.experimental.pallas import tpu as pltpu
from jax.sharding import Mesh, PartitionSpec as P

ITERS = 4
RANK = 96
LANES = 128
HIGHEST = lax.Precision.HIGHEST


def dot(a, b, contract, precision=HIGHEST):
    return lax.dot_general(
        a, b, (contract, ((), ())), precision=precision, preferred_element_type=jnp.float32
    )


def invert_factors(works):
    eight = (8, LANES)
    sublane = lax.broadcasted_iota(jnp.int32, eight, 0)
    lane = lax.broadcasted_iota(jnp.int32, eight, 1)
    for top in range(0, RANK, 8):
        inside = (lane >= top) & (lane < top + 8)
        for work in works:
            panel = work[top : top + 8, :]
            a = {
                (i, j): jnp.broadcast_to(panel[i : i + 1, top + j : top + j + 1], eight)
                for i in range(8)
                for j in range(i + 1)
            }
            inverse = []
            for j in range(8):
                inverse.append(1.0 / a[j, j])
                for i in range(j + 1, 8):
                    factor = a[i, j] * inverse[j]
                    for k in range(j + 1, i + 1):
                        a[i, k] = a[i, k] - factor * a[k, j]
            opened = jnp.where(inside, jnp.where(lane == top + sublane, 1.0, 0.0), panel)
            rows = [jnp.broadcast_to(opened[i : i + 1], eight) for i in range(8)]
            done = rows[0] * lax.rsqrt(a[0, 0])
            for j in range(8):
                if j > 0:
                    done = jnp.where(sublane == j, rows[j] * lax.rsqrt(a[j, j]), done)
                for i in range(j + 1, 8):
                    rows[i] = rows[i] - (a[i, j] * inverse[j]) * rows[j]
            work[top : top + 8, :] = done
            if top + 8 == RANK:
                continue
            held = work[top + 8 : top + 16, :]
            column = [jnp.broadcast_to(held[:, top + j : top + j + 1], eight) for j in range(8)]
            held = jnp.where(inside, 0.0, held)
            for j in range(8):
                factor = column[j] * inverse[j]
                for k in range(j + 1, 8):
                    column[k] = column[k] - factor * a[k, j]
                held = held - factor * rows[j]
            work[top + 8 : top + 16, :] = held
            if top + 16 < RANK and len(works) > 1:
                change = dot(done, done, ((0,), (0,)))
                for row in range(top + 16, RANK, 8):
                    rest = jnp.where(inside, 0.0, work[row : row + 8, :])
                    work[row : row + 8, :] = rest - change[row : row + 8, :]
            elif top + 16 < RANK:
                for row in range(top + 16, RANK, 8):
                    held = work[row : row + 8, :]
                    column = [jnp.broadcast_to(held[:, top + j : top + j + 1], eight) for j in range(8)]
                    held = jnp.where(inside, 0.0, held)
                    for j in range(8):
                        factor = column[j] * inverse[j]
                        for k in range(j + 1, 8):
                            column[k] = column[k] - factor * a[k, j]
                        held = held - factor * rows[j]
                    work[row : row + 8, :] = held


def iterate(grams, images, works):
    row = lax.broadcasted_iota(jnp.int32, (RANK, LANES), 0)
    column = lax.broadcasted_iota(jnp.int32, (RANK, LANES), 1)
    lower = row >= column
    empty = jnp.zeros((LANES - RANK, LANES), jnp.float32)

    def turn(index, carry):
        now, later = lax.rem(index, 2), lax.rem(index + 1, 2)
        for image, work in zip(images, works):
            held = image[now]
            work[...] = dot(held, held, ((0,), (0,)))[:RANK]
        ahead = [dot(gram[...], image[now], ((1,), (0,))) for gram, image in zip(grams, images)]
        invert_factors(works)
        for image, work, product in zip(images, works, ahead):
            inverse = jnp.concatenate([jnp.where(lower, work[...], 0.0), empty], axis=0)
            image[later] = dot(product, inverse, ((1,), (1,)))
        return carry

    lax.fori_loop(0, ITERS, turn, 0)
    found = []
    for image, work in zip(images, works):
        inverse = jnp.concatenate([jnp.where(lower, work[...], 0.0), empty], axis=0)
        found.append(dot(image[(ITERS - 1) % 2], inverse, ((1,), (1,))))
    return found


def solver_body(
    row_total, place_ref, own_ref, other_ref, coef_ref, energy_ref, gram_a, gram_b, image_a, image_b,
    work_a, work_b, gram_c, image_c, gram_ref,
):
    half = 2 * RANK
    first = place_ref[1] == 0
    count = 0
    for i in range(3):
        for j in range(i, 3):
            here = slice(LANES * (count % 3), LANES * (count % 3 + 1))
            own, other = own_ref[here, :], other_ref[here, :]
            tile = jnp.where(first, own, other) if count < 3 else jnp.where(first, other, own)
            gram_ref[LANES * i : LANES * (i + 1), LANES * j : LANES * (j + 1)] = tile
            if i != j:
                gram_ref[LANES * j : LANES * (j + 1), LANES * i : LANES * (i + 1)] = tile.T
            count += 1
    lane = lax.broadcasted_iota(jnp.int32, (half, LANES), 1)
    for index, (gram, image) in enumerate(((gram_a, image_a), (gram_b, image_b))):
        block = gram_ref[half * index : half * index + half, half * index : half * index + half]
        gram[...] = block
        image[0] = jnp.where(lane < RANK, block[:, :LANES], 0.0)
    first_a, first_b = [
        found.astype(jnp.bfloat16)
        for found in iterate((gram_a, gram_b), (image_a, image_b), (work_a, work_b))
    ]
    wide_a, wide_b = first_a.astype(jnp.float32), first_b.astype(jnp.float32)
    side_a = dot(gram_a[...], wide_a, ((1,), (0,)))
    side_b = dot(gram_b[...], wide_b, ((1,), (0,)))
    cross = dot(gram_ref[half:, :half], wide_a, ((1,), (0,)))
    low_left = dot(wide_b, cross, ((0,), (0,)))
    gram_c[:LANES, :LANES] = dot(wide_a, side_a, ((0,), (0,)))
    gram_c[LANES:, LANES:] = dot(wide_b, side_b, ((0,), (0,)))
    gram_c[LANES:, :LANES] = low_left
    gram_c[:LANES, LANES:] = low_left.T
    image_c[0] = gram_c[:, :LANES]
    (final,) = iterate((gram_c,), (image_c,), (work_a,))
    energy = dot(final, dot(gram_c[...], final, ((1,), (0,))), ((0,), (0,)))
    energy_ref[...] = energy[:RANK, :RANK] * (1.0 / row_total)
    second = final.astype(jnp.bfloat16)
    coef_ref[:, :half] = dot(second[:LANES], first_a, ((0,), (1,)), None)[:RANK].astype(jnp.bfloat16)
    coef_ref[:, half:] = dot(second[LANES:], first_b, ((0,), (1,)), None)[:RANK].astype(jnp.bfloat16)


def solve(halves, places, row_total):
    f32 = jnp.float32
    half, wide = 2 * RANK, 2 * LANES
    return pl.pallas_call(
        functools.partial(solver_body, row_total),
        out_shape=(
            jax.ShapeDtypeStruct((RANK, 2 * half), jnp.bfloat16),
            jax.ShapeDtypeStruct((RANK, RANK), f32),
        ),
        in_specs=[pl.BlockSpec(memory_space=pltpu.SMEM)] + [pl.BlockSpec(memory_space=pltpu.VMEM)] * 2,
        out_specs=(pl.BlockSpec(memory_space=pltpu.VMEM),) * 2,
        scratch_shapes=[
            pltpu.VMEM((half, half), f32), pltpu.VMEM((half, half), f32),
            pltpu.VMEM((2, half, LANES), f32), pltpu.VMEM((2, half, LANES), f32),
            pltpu.VMEM((RANK, LANES), f32), pltpu.VMEM((RANK, LANES), f32),
            pltpu.VMEM((wide, wide), f32), pltpu.VMEM((2, wide, LANES), f32),
            pltpu.VMEM((2 * half, 2 * half), f32),
        ],
        compiler_params=pltpu.CompilerParams(vmem_limit_bytes=32 * 1024 * 1024),
        name="solver",
    )(places, *halves)


def pair_swap(x, axis):
    return lax.ppermute(x, axis, [(0, 1), (1, 0)])


def shifted(x, axis, step):
    n = lax.axis_size(axis)
    return lax.ppermute(x, axis, [(i, (i + step) % n) for i in range(n)])


def sum_halves(keep, give, riders):
    part = keep + pair_swap(give, "core")
    n = lax.axis_size("x")
    me = lax.axis_index("x")
    pieces = part.reshape(n, part.shape[0] // n, part.shape[1])

    def piece(step):
        return lax.dynamic_index_in_dim(pieces, (me + step) % n, 0, keepdims=False)

    mine = sum([shifted(piece(step), "x", step) for step in range(1, n)], piece(0))
    mine = mine + pair_swap(mine, "z_lo")
    with jax.named_scope("ring_sum"):
        got = [shifted(mine, "z_hi", step) for step in range(1, lax.axis_size("z_hi"))]
    got, riders = lax.optimization_barrier((got, riders))
    mine = sum(got, mine)
    got = [mine] + [shifted(mine, "x", step) for step in range(1, n)]
    part = jnp.stack(got)[(me - jnp.arange(n)) % n].reshape(part.shape)
    return (part, pair_swap(part, "core")), riders


def cut(whole, starts, width):
    return [lax.dynamic_slice_in_dim(whole, start * width, width, 1) for start in starts]


def place(pieces, starts, whole):
    width = pieces[0].shape[1]
    for piece, start in zip(pieces, starts):
        whole = lax.dynamic_update_slice_in_dim(whole, piece, start * width, 1)
    return whole


PAIRS = [(i, j) for i in range(3) for j in range(i, 3)]


def ring_row(place_ref, step, rank):
    return pl.multiple_of(lax.rem(place_ref[0] + step, 4) * rank, 32)


def add_gram(first, width, place_ref, pieces, held, total_ref):
    rank, columns = pieces[0].shape
    for step in range(columns // width):
        for index in range(4):
            spot = pl.ds(ring_row(place_ref, index, rank), rank)
            held[step % 2, spot, :] = pieces[index][:, width * step : width * step + width]
        rows = held[step % 2]
        product = lax.dot_general(
            rows, rows, (((1,), (1,)), ((), ())), preferred_element_type=jnp.float32
        )
        total_ref[...] = product if first and step == 0 else total_ref[...] + product


def first_gram_body(width, place_ref, *refs):
    pieces, total_ref, held = refs[:4], *refs[4:]
    add_gram(True, width, place_ref, pieces, held, total_ref)


def last_gram_body(width, place_ref, before_ref, *refs):
    pieces, keep_ref, give_ref, held, total = refs[:4], *refs[4:]
    total[...] = before_ref[...]
    add_gram(False, width, place_ref, pieces, held, total)
    first = place_ref[1] == 0
    for index in range(3):
        (i, j), (k, m) = PAIRS[index], PAIRS[index + 3]
        low = total[LANES * i : LANES * (i + 1), LANES * j : LANES * (j + 1)]
        high = total[LANES * k : LANES * (k + 1), LANES * m : LANES * (m + 1)]
        here = slice(LANES * index, LANES * (index + 1))
        keep_ref[here, :] = jnp.where(first, low, high)
        give_ref[here, :] = jnp.where(first, high, low)


def local_gram(pieces, places, before=None):
    rank, columns = pieces[0].shape
    width = min(columns, 2048)
    square = jax.ShapeDtypeStruct((4 * rank, 4 * rank), jnp.float32)
    half = jax.ShapeDtypeStruct((3 * LANES, LANES), jnp.float32)
    whole = pl.BlockSpec(memory_space=pltpu.VMEM)
    held = pltpu.VMEM((2, 4 * rank, width), jnp.bfloat16)
    start = before is None
    operands = list(pieces) if start else [before, *pieces]
    return pl.pallas_call(
        functools.partial(first_gram_body if start else last_gram_body, width),
        out_shape=square if start else (half, half),
        in_specs=[pl.BlockSpec(memory_space=pltpu.SMEM)] + [whole] * len(operands),
        out_specs=whole if start else (whole, whole),
        scratch_shapes=[held] if start else [held, pltpu.VMEM(square.shape, jnp.float32)],
        cost_estimate=pl.CostEstimate(
            flops=32 * rank * rank * columns, bytes_accessed=8 * rank * columns, transcendentals=0
        ),
        compiler_params=pltpu.CompilerParams(vmem_limit_bytes=48 * 1024 * 1024),
        name="local_gram",
    )(places, *operands)


def merge_body(sets, width, place_ref, coef_ref, *refs):
    pieces, outs, held = refs[: 4 * sets], refs[4 * sets : -1], refs[-1]
    rank, columns = pieces[0].shape
    slot = 0
    for index in range(sets):
        for step in range(columns // width):
            here = slice(width * step, width * step + width)
            for row in range(4):
                spot = pl.ds(ring_row(place_ref, row, rank), rank)
                held[slot, spot, :] = pieces[4 * index + row][:, here]
            outs[index][:, here] = jnp.dot(
                coef_ref[...], held[slot], preferred_element_type=jnp.float32
            ).astype(jnp.bfloat16)
            slot = 1 - slot


def merge(coef, sets, places):
    count = len(sets)
    rank, columns = sets[0][0].shape
    width = min(columns, 1024)
    whole = pl.BlockSpec(memory_space=pltpu.VMEM)
    return pl.pallas_call(
        functools.partial(merge_body, count, width),
        out_shape=(jax.ShapeDtypeStruct((rank, columns), jnp.bfloat16),) * count,
        in_specs=[pl.BlockSpec(memory_space=pltpu.SMEM)] + [whole] * (1 + 4 * count),
        out_specs=(whole,) * count,
        scratch_shapes=[pltpu.VMEM((2, 4 * rank, width), jnp.bfloat16)],
        cost_estimate=pl.CostEstimate(
            flops=8 * count * rank * rank * columns,
            bytes_accessed=10 * count * rank * columns,
            transcendentals=0,
        ),
        compiler_params=pltpu.CompilerParams(vmem_limit_bytes=48 * 1024 * 1024),
        name="merge",
    )(places, coef, *[piece for pieces in sets for piece in pieces])


def up(x):
    return shifted(x, "z_hi", 1)


def down(x):
    return shifted(x, "z_hi", -1)


def local(factors):
    own = factors[0]
    rank, columns = own.shape
    row_total = columns * lax.axis_size(("x", "z_lo", "core"))
    me = lax.axis_index("z_hi")
    width = columns // 8

    def spot(step, half):
        return (me + step) % 4 * 2 + half

    def part(*spots):
        return cut(own, [spot(*s) for s in spots], width)

    far_down, far_up = part((2, 0), (1, 1))
    a2 = down(far_down)
    b2 = up(far_up)
    own, far_down, far_up = lax.optimization_barrier((own, far_down, far_up))
    below_first, above_second = part((3, 0), (0, 1))
    a1 = down(below_first)
    b1 = up(above_second)
    merged = jnp.zeros((rank, columns), jnp.bfloat16)
    a2, own_late, merged = lax.optimization_barrier((a2, own, merged))
    below_second, kept_first, kept_second = cut(
        own_late, [spot(2, 1), spot(0, 0), spot(3, 1)], width
    )
    a4 = down(a2)
    a3 = down(below_second)
    b2, own_late = lax.optimization_barrier((b2, own))
    (above_first,) = cut(own_late, [spot(1, 0)], width)
    b4 = up(b2)
    b3 = up(above_first)
    places = jnp.stack([me, lax.axis_index("core")]).astype(jnp.int32)
    before = local_gram([kept_first, a1, a4, b3], places)
    halves = local_gram([kept_second, a3, b4, b1], places, before)
    halves, (kept_first, kept_second, b3, a3) = sum_halves(
        *halves, (kept_first, kept_second, b3, a3)
    )
    with jax.named_scope("second_holder"):
        c1 = up(kept_first)
        c3 = down(kept_second)
        c2 = up(b3)
        c4 = down(a3)
    coef, energy = solve(halves, places, float(row_total))
    coef, c1, c3 = lax.optimization_barrier((coef, c1, c3))
    upper_first, lower_second = merge(
        coef, [[kept_first, a1, a4, b3], [kept_second, a3, b4, b1]], places
    )
    with jax.named_scope("result"):
        sent_first, sent_second = down(upper_first), up(lower_second)
    upper_second, lower_first = merge(
        coef, [[above_second, c3, c4, b2], [below_first, a2, c2, c1]], places
    )
    with jax.named_scope("result"):
        sent = [sent_first, sent_second, up(lower_first), down(upper_second)]
    merged = place(sent[:2], [spot(1, 0), spot(2, 1)], merged)
    merged = place(
        [upper_first, upper_second, lower_first, lower_second],
        [spot(0, 0), spot(0, 1), spot(3, 0), spot(3, 1)],
        merged,
    )
    merged = place(sent[2:], [spot(2, 0), spot(1, 1)], merged)
    return (merged[None], energy[None])


def solution(mesh):
    sizes = mesh.devices.size // 64
    fine = Mesh(mesh.devices.reshape(sizes, 4, 4, 2, 2), ("y", "z_hi", "x", "z_lo", "core"))
    group, space = ("y", "z_hi"), ("x", "z_lo", "core")
    return jax.shard_map(
        local,
        mesh=fine,
        in_specs=(P(group, None, space),),
        out_specs=(P(group, None, space), P(group, None, None)),
        check_vma=False,
    )
```
